32 devices in a mesh: groups: 2 (over y), feat: 16 (over z, x, core).
Axes of the slice: x: 2, y: 2, z: 4, core: 2. Of those that a mesh axis runs over, the one named last changes fastest.
Arguments:
- residual: bfloat16 [2, 256, 8192], P(None, ('groups', 'feat')), parts along dimension 1, may hold values from -6 to 6
- feature_ids: int32 [2, 256, 64], P(None, 'groups'), parts along dimension 1, may hold values from 0 to 2047, as said below
- activations: bfloat16 [2, 256, 64], P(None, 'groups'), parts along dimension 1, may hold values from 0.5 to 8
- decoder: bfloat16 [4096, 8192], P(('groups', 'feat')), parts along dimension 0, may hold values from -0.0625 to 0.0625
- bias: bfloat16 [16384], P('groups'), parts along dimension 0, may hold values from -5 to 5
Outputs:
- weight_grad: bfloat16 [4096, 8192], P(('groups', 'feat')), parts along dimension 0
- code_grad: float32 [2, 256, 64], P(None, 'groups'), parts along dimension 1
The draws below stay inside these ranges and needn't reach their ends.
There are 2 independent parts, one for each index of `groups`. The reference program is written for one: setup_inputs(seed, part) draws one part's arguments, and reference() takes and returns one part's arrays. A program takes and returns all parts, laid end to end along the dimension named above; each array names one. Nothing has to cross between parts.
Inputs may be any that keep to these rules, and one draw needn't show every extreme that they name: `feature_ids`: each token's 64 feature numbers are distinct; both ends of the range are used. `feature_ids`: in each micro-batch, the 512 feature numbers of the tokens i * 8 to (i + 1) * 8 - 1 are distinct, and at most 64 of them lie in one run of 128 numbers f * 128 to (f + 1) * 128 - 1; every such group of tokens reaches 64 in some run.
All inputs are finite; a program needn't handle non-finite values.
Results may differ from the reference program's by a relative error of at most 0.0034.
Values may be sent and summed in bfloat16 or wider, within the bound.
A program may use at most 64 MiB of HBM per device.

```python
import math
import jax
import jax.numpy as jnp
from jax import lax

D = 8192
K = 64
FEAT_DEV = 128
MB = 2
TOK_MB = 128
FEATURES = 2048
SHARE = 8
ROUTE_CAP = 64
N_FEAT = 16


def draw_block(block_key, block_number, last_block):
    hot_key, base_key, order_key, place_key = jax.random.split(block_key, 4)
    pool_size = N_FEAT * ROUTE_CAP
    hot = jax.random.randint(hot_key, (), 0, N_FEAT).astype(jnp.int32)
    hot = jnp.where(block_number == 0, 0, jnp.where(block_number == last_block, N_FEAT - 1, hot)).astype(jnp.int32)
    bases = jax.random.randint(base_key, (N_FEAT,), 0, FEAT_DEV).astype(jnp.int32)
    hot_base = jnp.where(block_number == 0, 0, jnp.where(block_number == last_block, FEAT_DEV - ROUTE_CAP, bases[hot])).astype(jnp.int32)
    shard_index = jnp.arange(N_FEAT, dtype=jnp.int32)
    bases = jnp.where(shard_index == hot, hot_base, bases).astype(jnp.int32)
    pool = jnp.arange(pool_size, dtype=jnp.int32)
    pool_shard = pool // ROUTE_CAP
    pool_copy = pool % ROUTE_CAP
    order = jax.random.permutation(order_key, pool_size).astype(jnp.int32)
    score = jnp.where(pool_shard == hot, -1, order).astype(jnp.int32)
    chosen = jnp.argsort(score, stable=True)[:SHARE * K].astype(jnp.int32)
    chosen = chosen[jax.random.permutation(place_key, SHARE * K)].astype(jnp.int32)
    shard = pool_shard[chosen]
    copy_number = pool_copy[chosen]
    local = (bases[shard] + copy_number) % FEAT_DEV
    return (shard * FEAT_DEV + local).astype(jnp.int32).reshape(SHARE, K)


def draw_feature_ids(key, part):
    key = jax.random.fold_in(key, 11)
    block_count = MB * N_FEAT
    block_keys = jax.random.split(key, block_count)
    numbers = jnp.arange(block_count, dtype=jnp.int32)
    picked = jax.vmap(lambda block_key, number: draw_block(block_key, number, block_count - 1))(block_keys, numbers)
    return picked.reshape(MB, TOK_MB, K).astype(jnp.int32)


def levels(own_key, dims, cuts, least, top_value):
    factor_of, own = 1.0, jax.random.fold_in(own_key, 6)
    for dim, blocks in cuts:
        steps = jnp.exp(jax.random.uniform(jax.random.fold_in(own, dim), (blocks,), jnp.float32, least / len(cuts), top_value / len(cuts)))
        factor_of = factor_of * jnp.repeat(steps, dims[dim] // blocks).reshape([-1 if axis == dim else 1 for axis in range(len(dims))])
    return factor_of


def gaussian(own_key, shape, deviation, limit, pieces=(), held_as=jnp.bfloat16):
    array = deviation * jax.random.normal(own_key, shape, jnp.float32)
    if pieces:
        array = array * levels(own_key, shape, pieces, -0.22, 0.18)
    return jnp.clip(array, -limit, limit).astype(held_as)


def setup_inputs(seed: int = 0, part: int = 0) -> dict:
    splits = jax.random.split(jax.random.key(seed), 6)
    part_keys = jax.random.split(jax.random.fold_in(splits[5], part), 6)
    residual = gaussian(part_keys[0], (MB, TOK_MB, D), 1.0, 6.0, ((1, 16),))
    feature_ids = draw_feature_ids(jax.random.fold_in(jax.random.fold_in(splits[5], part), 71), part)
    activations = jnp.clip(jnp.exp(jax.random.uniform(part_keys[2], (MB, TOK_MB, K), jnp.float32, math.log(0.5), math.log(8.0))), 0.5, 8.0).astype(jnp.bfloat16)
    decoder = gaussian(part_keys[3], (FEATURES, D), D ** -0.5, 0.0625, ((0, 16),))
    bias = gaussian(part_keys[4], (D,), 1.0, 5.0)
    return {"residual": residual, "feature_ids": feature_ids, "activations": activations, "decoder": decoder, "bias": bias}


def reference(residual, feature_ids, activations, decoder, bias):
    def one_batch(total, inputs):
        ids, acts, target = inputs
        rows = decoder[ids].astype(jnp.float32)
        recon = jnp.einsum("tk,tkd->td", acts.astype(jnp.float32), rows) + bias.astype(jnp.float32)
        error = (recon - target.astype(jnp.float32)).astype(jnp.bfloat16)
        error_wide = error.astype(jnp.float32)
        code_grad = jnp.einsum("td,tkd->tk", error_wide, rows)
        terms = acts.astype(jnp.float32)[:, :, None] * error_wide[:, None, :]
        total = total.at[ids.reshape(-1)].add(terms.reshape(-1, D))
        return total, code_grad

    start_total = jnp.zeros((FEATURES, D), jnp.float32)
    total, code_grad = lax.scan(one_batch, start_total, (feature_ids, activations, residual))
    return total.astype(jnp.bfloat16), code_grad
```

```python
import jax
import jax.numpy as jnp
from jax import lax
from jax.experimental import pallas as pl
from jax.experimental.pallas import tpu as pltpu
from jax.sharding import PartitionSpec as P

MESH = pl.DeviceIdType.MESH
PLANES = 4
QUARTERS = 4
DEVICES = PLANES * QUARTERS
CHUNKS = 4
SUM_TYPE = jnp.float32


def fused_kernel(
    ids_ref,
    acts_ref,
    res_ref,
    dec_in,
    bias_ref,
    wg_out,
    cg_out,
    dec,
    part,
    got1,
    got2,
    err,
    wg,
    res,
    codes,
    codes_t,
    back,
    pick,
    cg_got,
    own_sem,
    dec_send,
    dec_recv,
    res_send,
    res_recv,
    sum_send,
    sum_recv,
    wg_send,
    wg_recv,
    wg_own,
    cg_send,
    cg_recv,
):
    feat = dec_in.shape[0]
    width = dec_in.shape[1] // QUARTERS
    step = width // CHUNKS
    tokens = codes.shape[0]
    half, quarter = tokens // 2, tokens // 4
    share = res_ref.shape[0]
    lanes = ids_ref.shape[1]
    top_k = lanes // 2
    rows8 = share // 2

    me = lax.axis_index("feat")
    z, q = lax.div(me, QUARTERS), lax.rem(me, QUARTERS)
    z_hi, z_lo = lax.div(z, 2), lax.rem(z, 2)
    near = (z + 1 - 2 * z_lo) * QUARTERS + q
    far = lax.rem(z + 2, PLANES) * QUARTERS + q
    mates = [lax.rem(q + r, QUARTERS) for r in range(QUARTERS)]

    def span(start, size):
        return pl.ds(pl.multiple_of(start, size), size)

    def remote(src, dst, send, recv, device):
        copy = pltpu.make_async_remote_copy(
            src_ref=src,
            dst_ref=dst,
            send_sem=send,
            recv_sem=recv,
            device_id={"feat": device},
            device_id_type=MESH,
        )
        copy.start()
        return copy

    barrier = pltpu.get_barrier_semaphore()
    for r in range(1, DEVICES):
        pl.semaphore_signal(
            barrier, inc=1, device_id={"feat": lax.rem(me + r, DEVICES)}, device_id_type=MESH
        )
    pl.semaphore_wait(barrier, DEVICES - 1)

    sends = []
    own_dec = pltpu.make_async_copy(
        dec_in.at[:, span(q * width, width)], dec.at[span(q * feat, feat), :], own_sem.at[0]
    )
    own_dec.start()
    own_res = pltpu.make_async_copy(
        res_ref.at[:, span(q * width, width)], res.at[span(q * share, share), :], own_sem.at[1]
    )
    own_res.start()
    dec_copies = {}
    res_copies = []
    for c in range(CHUNKS):
        for r in range(1, QUARTERS):
            dec_copies[c, r] = remote(
                dec_in.at[:, span(mates[r] * width + c * step, step)],
                dec.at[span(q * feat, feat), pl.ds(c * step, step)],
                dec_send.at[c, r],
                dec_recv.at[c, r],
                z * QUARTERS + mates[r],
            )
        if c == 0:
            for r in range(1, QUARTERS):
                res_copies.append(
                    remote(
                        res_ref.at[:, span(mates[r] * width, width)],
                        res.at[span(q * share, share), :],
                        res_send.at[r],
                        res_recv.at[r],
                        z * QUARTERS + mates[r],
                    )
                )
    sends += list(dec_copies.values()) + res_copies

    plane_feat = QUARTERS * feat
    first = z * plane_feat

    def row_of(i):
        zi, qi = lax.div(i, QUARTERS), lax.rem(i, QUARTERS)
        return pl.multiple_of((lax.rem(zi, 2) * 2 + lax.div(zi, 2)) * quarter + qi * share, share)

    @pl.loop(0, DEVICES)
    def _(i):
        rows = pl.ds(pl.multiple_of(i * rows8, rows8), rows8)
        ids8 = ids_ref[rows, :] - first
        acts8 = acts_ref[rows, :]
        feature = lax.broadcasted_iota(jnp.int32, (rows8, plane_feat), 1)
        blocks = []
        for batch in range(2):
            block = jnp.zeros((rows8, plane_feat), jnp.float32)
            for k in range(batch * top_k, (batch + 1) * top_k):
                block = jnp.where(ids8[:, k : k + 1] == feature, acts8[:, k : k + 1], block)
            blocks.append(block)
        both = jnp.concatenate(blocks, axis=0)
        codes[pl.ds(row_of(i), share), :] = both.astype(jnp.bfloat16)

    for f in range(QUARTERS):
        codes_t[f * feat : (f + 1) * feat, :] = (
            codes[:, f * feat : (f + 1) * feat].astype(jnp.float32).T.astype(jnp.bfloat16)
        )

    own_dec.wait()
    own_res.wait()

    mine_half = span(z_lo * half, half)
    other_half = span((1 - z_lo) * half, half)
    mine = span(z_lo * half + z_hi * quarter, quarter)
    other = span(z_lo * half + (1 - z_hi) * quarter, quarter)
    flying = {}

    def cols_of(c):
        return pl.ds(c * step, step)

    def project(c):
        cols = cols_of(c)
        for r in range(1, QUARTERS):
            dec_copies[c, r].wait_recv()
        part[:, cols] = jnp.dot(
            codes[...], dec[:, cols], preferred_element_type=jnp.float32
        ).astype(part.dtype)
        flying[0, c] = remote(
            part.at[other_half, cols], got1.at[:, cols], sum_send.at[0, c], sum_recv.at[0, c], near
        )

    def halve(c):
        cols = cols_of(c)
        flying[0, c].wait_recv()
        part[mine_half, cols] = part[mine_half, cols] + got1[:, cols]
        flying[1, c] = remote(
            part.at[other, cols], got2.at[:, cols], sum_send.at[1, c], sum_recv.at[1, c], far
        )

    def make_error(c):
        cols = cols_of(c)
        if c == 0:
            for copy in res_copies:
                copy.wait_recv()
        flying[1, c].wait_recv()
        recon = part[mine, cols] + got2[:, cols]
        shift = bias_ref[:, span(q * width + c * step, step)]
        err[mine, cols] = (recon + shift - res[:, cols].astype(jnp.float32)).astype(jnp.bfloat16)
        flying[2, c] = remote(
            err.at[mine, cols], err.at[mine, cols], sum_send.at[2, c], sum_recv.at[2, c], far
        )

    def spread(c):
        cols = cols_of(c)
        flying[2, c].wait_recv()
        flying[3, c] = remote(
            err.at[mine_half, cols],
            err.at[mine_half, cols],
            sum_send.at[3, c],
            sum_recv.at[3, c],
            near,
        )

    wg_copies = []
    wg_local = []

    def gradients(c):
        cols = cols_of(c)
        flying[3, c].wait_recv()
        wg[:, cols] = jnp.dot(
            codes_t[...], err[:, cols], preferred_element_type=jnp.float32
        ).astype(jnp.bfloat16)
        place = span(q * width + c * step, step)
        for r in range(1, QUARTERS):
            wg_copies.append(
                remote(
                    wg.at[span(mates[r] * feat, feat), cols],
                    wg_out.at[:, place],
                    wg_send.at[c, r],
                    wg_recv.at[c, r],
                    z * QUARTERS + mates[r],
                )
            )
        local = pltpu.make_async_copy(
            wg.at[span(q * feat, feat), cols], wg_out.at[:, place], wg_own.at[c]
        )
        local.start()
        wg_local.append(local)
        term = lax.dot_general(
            err[:, cols],
            dec[:, cols],
            (((1,), (1,)), ((), ())),
            preferred_element_type=jnp.float32,
        )
        back[...] = term if c == 0 else back[...] + term

    stages = (project, halve, make_error, spread, gradients)
    for tick in range(CHUNKS + len(stages) - 1):
        for number, stage in enumerate(stages):
            if 0 <= tick - number < CHUNKS:
                stage(tick - number)
    sends += list(flying.values()) + wg_copies

    @pl.loop(0, DEVICES)
    def _(i):
        rows = pl.ds(pl.multiple_of(i * rows8, rows8), rows8)
        ids8 = ids_ref[rows, :] - first
        lane = lax.broadcasted_iota(jnp.int32, (rows8, lanes), 1)
        row = row_of(i)
        value = jnp.zeros((rows8, lanes), jnp.float32)
        for f in range(plane_feat // lanes):
            at = ids8 - f * lanes
            inside = (at >= 0) & (at < lanes)
            at = jnp.clip(at, 0, lanes - 1)
            taken = []
            for batch in range(2):
                block = back[
                    pl.ds(pl.multiple_of(row + batch * rows8, rows8), rows8),
                    f * lanes : (f + 1) * lanes,
                ]
                taken.append(
                    jnp.take_along_axis(block, at, axis=1, mode="promise_in_bounds")
                )
            found = jnp.where(lane < top_k, taken[0], taken[1])
            value = jnp.where(inside, found, value)
        pick[rows, :] = value

    to_owner = []
    for r in range(1, DEVICES):
        owner = lax.rem(me + r, DEVICES)
        to_owner.append(
            remote(
                pick.at[span(owner * rows8, rows8), :],
                cg_got.at[r],
                cg_send.at[0, r],
                cg_recv.at[0, r],
                owner,
            )
        )
    for copy in to_owner:
        copy.wait_recv()
    my_rows = span(me * rows8, rows8)
    total = pick[my_rows, :]
    for r in range(1, DEVICES):
        total = total + cg_got[r]
    cg_out[my_rows, :] = total
    to_all = []
    for r in range(1, DEVICES):
        to_all.append(
            remote(
                cg_out.at[my_rows, :],
                cg_out.at[my_rows, :],
                cg_send.at[1, r],
                cg_recv.at[1, r],
                lax.rem(me + r, DEVICES),
            )
        )
    for copy in to_all + wg_copies:
        copy.wait_recv()
    for copy in wg_local:
        copy.wait()
    for copy in sends + to_owner + to_all:
        copy.wait_send()


def fused(residual, feature_ids, activations, decoder, bias):
    feat, model_width = decoder.shape
    batches, share_rows = residual.shape[0], residual.shape[1]
    tokens = feature_ids.shape[1]
    width = model_width // QUARTERS
    rows = batches * tokens
    ids = jnp.concatenate([feature_ids[0], feature_ids[1]], axis=1)
    acts = jnp.concatenate([activations[0], activations[1]], axis=1).astype(jnp.float32)
    lanes = ids.shape[1]
    vmem = pl.BlockSpec(memory_space=pltpu.VMEM)
    hbm = pl.BlockSpec(memory_space=pl.ANY)
    weight_grad, grads = pl.pallas_call(
        fused_kernel,
        out_shape=(
            jax.ShapeDtypeStruct((feat, model_width), jnp.bfloat16),
            jax.ShapeDtypeStruct((tokens, lanes), jnp.float32),
        ),
        in_specs=[vmem, vmem, vmem, hbm, vmem],
        out_specs=(hbm, vmem),
        scratch_shapes=[
            pltpu.VMEM((QUARTERS * feat, width), jnp.bfloat16),
            pltpu.VMEM((rows, width), SUM_TYPE),
            pltpu.VMEM((rows // 2, width), SUM_TYPE),
            pltpu.VMEM((rows // 4, width), SUM_TYPE),
            pltpu.VMEM((rows, width), jnp.bfloat16),
            pltpu.VMEM((QUARTERS * feat, width), jnp.bfloat16),
            pltpu.VMEM((rows // 4, width), jnp.bfloat16),
            pltpu.VMEM((rows, QUARTERS * feat), jnp.bfloat16),
            pltpu.VMEM((QUARTERS * feat, rows), jnp.bfloat16),
            pltpu.VMEM((rows, QUARTERS * feat), jnp.float32),
            pltpu.VMEM((tokens, lanes), jnp.float32),
            pltpu.VMEM((DEVICES, share_rows, lanes), jnp.float32),
            pltpu.SemaphoreType.DMA((2,)),
            pltpu.SemaphoreType.DMA((CHUNKS, QUARTERS)),
            pltpu.SemaphoreType.DMA((CHUNKS, QUARTERS)),
            pltpu.SemaphoreType.DMA((QUARTERS,)),
            pltpu.SemaphoreType.DMA((QUARTERS,)),
            pltpu.SemaphoreType.DMA((4, CHUNKS)),
            pltpu.SemaphoreType.DMA((4, CHUNKS)),
            pltpu.SemaphoreType.DMA((CHUNKS, QUARTERS)),
            pltpu.SemaphoreType.DMA((CHUNKS, QUARTERS)),
            pltpu.SemaphoreType.DMA((CHUNKS,)),
            pltpu.SemaphoreType.DMA((2, DEVICES)),
            pltpu.SemaphoreType.DMA((2, DEVICES)),
        ],
        compiler_params=pltpu.CompilerParams(
            collective_id=0, has_side_effects=True, vmem_limit_bytes=40 * 2**20
        ),
        name="fused_backward",
    )(
        ids,
        acts,
        residual.reshape(batches * share_rows, model_width),
        decoder,
        bias.astype(jnp.float32).reshape(1, model_width),
    )
    code_grad = grads.reshape(tokens, batches, lanes // batches).transpose(1, 0, 2)
    return weight_grad, code_grad


def local_codes(ids_block, acts_block, first_feature, feat_count):
    matches = (ids_block - first_feature)[:, :, None] == lax.iota(jnp.int32, feat_count)[
        None, None, :
    ]
    dense = jnp.einsum(
        "tkf,tk->tf", matches.astype(jnp.bfloat16), acts_block, preferred_element_type=jnp.float32
    )
    return dense.astype(jnp.bfloat16)


def pick_owned(backward, ids_block, first_feature, feat_count):
    local_ids = ids_block - first_feature
    owned = (local_ids >= 0) & (local_ids < feat_count)
    taken = jnp.take_along_axis(backward, jnp.clip(local_ids, 0, feat_count - 1), axis=1)
    return jnp.where(owned, taken, jnp.float32(0.0))


def error_products(codes, errors_all, decoder):
    weight_term = jnp.einsum("tf,td->fd", codes, errors_all, preferred_element_type=jnp.float32)
    backward = jnp.einsum("td,fd->tf", errors_all, decoder, preferred_element_type=jnp.float32)
    return (weight_term, backward)


def local(residual, feature_ids, activations, decoder, bias):
    feat_count, model_width = decoder.shape
    batches, share_rows = (residual.shape[0], residual.shape[1])
    first_feature = lax.axis_index("feat") * feat_count
    bias_wide = bias.astype(jnp.float32)
    accum = jnp.zeros((feat_count, model_width), jnp.float32)
    codes_list = [
        local_codes(feature_ids[batch], activations[batch], first_feature, feat_count)
        for batch in range(batches)
    ]
    picks = []
    for batch in range(batches):
        codes = codes_list[batch]

        def project(begin, number, codes=codes):
            return jnp.dot(codes, decoder, preferred_element_type=jnp.float32)

        recon = lax.psum_scatter(
            project(jnp.int32(0), share_rows * lax.axis_size("feat")),
            "feat",
            scatter_dimension=0,
            tiled=True,
        )
        error_share = (recon + bias_wide - residual[batch].astype(jnp.float32)).astype(jnp.bfloat16)
        errors_all = lax.all_gather(error_share, "feat", axis=0, tiled=True)
        weight_term, backward = error_products(codes, errors_all, decoder)
        accum = accum + weight_term
        picks.append(pick_owned(backward, feature_ids[batch], first_feature, feat_count))
    code_grad = lax.psum(jnp.stack(picks), "feat")
    return (accum.astype(jnp.bfloat16), code_grad)


def solution(mesh):
    placed = (
        P(None, ("groups", "feat"), None),
        P(None, "groups", None),
        P(None, "groups", None),
        P(("groups", "feat"), None),
        P("groups"),
    )
    return jax.shard_map(
        fused if mesh.shape["feat"] == DEVICES else local,
        mesh=mesh,
        in_specs=placed,
        out_specs=(P(("groups", "feat"), None), P(None, "groups", None)),
        check_vma=False,
    )
```

```python
import jax
import jax.numpy as jnp
from jax import lax
from jax.experimental import pallas as pl
from jax.experimental.pallas import tpu as pltpu
from jax.sharding import PartitionSpec as P

MESH = pl.DeviceIdType.MESH
PLANES = 4
QUARTERS = 4
DEVICES = PLANES * QUARTERS
CHUNKS = 8
LAGS = (0, 1, 2, 3, 4)
SUM_TYPE = jnp.float32


def fused_kernel(
    ids_ref,
    acts_ref,
    res_ref,
    dec_in,
    bias_ref,
    wg_out,
    cg_out,
    dec,
    part,
    got1,
    got2,
    err,
    wg,
    res,
    codes,
    codes_t,
    back,
    pick,
    cg_got,
    own_sem,
    dec_send,
    dec_recv,
    res_send,
    res_recv,
    sum_send,
    sum_recv,
    wg_send,
    wg_recv,
    wg_own,
    cg_send,
    cg_recv,
):
    feat = dec_in.shape[0]
    width = dec_in.shape[1] // QUARTERS
    step = width // CHUNKS
    tokens = codes.shape[0]
    half, quarter = tokens // 2, tokens // 4
    share = res_ref.shape[0]
    lanes = ids_ref.shape[1]
    top_k = lanes // 2
    rows8 = share // 2

    me = lax.axis_index("feat")
    z, q = lax.div(me, QUARTERS), lax.rem(me, QUARTERS)
    z_hi, z_lo = lax.div(z, 2), lax.rem(z, 2)
    near = (z + 1 - 2 * z_lo) * QUARTERS + q
    far = lax.rem(z + 2, PLANES) * QUARTERS + q
    mates = [lax.rem(q + r, QUARTERS) for r in range(QUARTERS)]

    def span(start, size):
        return pl.ds(pl.multiple_of(start, size), size)

    def remote(src, dst, send, recv, device):
        copy = pltpu.make_async_remote_copy(
            src_ref=src,
            dst_ref=dst,
            send_sem=send,
            recv_sem=recv,
            device_id={"feat": device},
            device_id_type=MESH,
        )
        copy.start()
        return copy

    barrier = pltpu.get_barrier_semaphore()
    for r in range(1, DEVICES):
        pl.semaphore_signal(
            barrier, inc=1, device_id={"feat": lax.rem(me + r, DEVICES)}, device_id_type=MESH
        )
    pl.semaphore_wait(barrier, DEVICES - 1)

    sends = []
    own_dec = pltpu.make_async_copy(
        dec_in.at[:, span(q * width, width)], dec.at[span(q * feat, feat), :], own_sem.at[0]
    )
    own_dec.start()
    own_res = pltpu.make_async_copy(
        res_ref.at[:, span(q * width, width)], res.at[span(q * share, share), :], own_sem.at[1]
    )
    own_res.start()
    dec_copies = {}
    res_copies = []
    for c in range(CHUNKS):
        for r in range(1, QUARTERS):
            dec_copies[c, r] = remote(
                dec_in.at[:, span(mates[r] * width + c * step, step)],
                dec.at[span(q * feat, feat), pl.ds(c * step, step)],
                dec_send.at[c, r],
                dec_recv.at[c, r],
                z * QUARTERS + mates[r],
            )
        if c == 0:
            for r in range(1, QUARTERS):
                res_copies.append(
                    remote(
                        res_ref.at[:, span(mates[r] * width, width)],
                        res.at[span(q * share, share), :],
                        res_send.at[r],
                        res_recv.at[r],
                        z * QUARTERS + mates[r],
                    )
                )
    sends += list(dec_copies.values()) + res_copies

    plane_feat = QUARTERS * feat
    first = z * plane_feat

    def row_of(i):
        zi, qi = lax.div(i, QUARTERS), lax.rem(i, QUARTERS)
        return pl.multiple_of((lax.rem(zi, 2) * 2 + lax.div(zi, 2)) * quarter + qi * share, share)

    @pl.loop(0, DEVICES)
    def _(i):
        rows = pl.ds(pl.multiple_of(i * rows8, rows8), rows8)
        ids8 = ids_ref[rows, :] - first
        acts8 = acts_ref[rows, :]
        feature = lax.broadcasted_iota(jnp.int32, (rows8, plane_feat), 1)
        blocks = []
        for batch in range(2):
            block = jnp.zeros((rows8, plane_feat), jnp.float32)
            for k in range(batch * top_k, (batch + 1) * top_k):
                block = jnp.where(ids8[:, k : k + 1] == feature, acts8[:, k : k + 1], block)
            blocks.append(block)
        both = jnp.concatenate(blocks, axis=0)
        codes[pl.ds(row_of(i), share), :] = both.astype(jnp.bfloat16)

    own_dec.wait()
    own_res.wait()

    mine_half = span(z_lo * half, half)
    other_half = span((1 - z_lo) * half, half)
    mine = span(z_lo * half + z_hi * quarter, quarter)
    other = span(z_lo * half + (1 - z_hi) * quarter, quarter)
    flying = {}

    def cols_of(c):
        return pl.ds(c * step, step)

    def project(c):
        cols = cols_of(c)
        for r in range(1, QUARTERS):
            dec_copies[c, r].wait_recv()
        part[:, cols] = jnp.dot(
            codes[...], dec[:, cols], preferred_element_type=jnp.float32
        ).astype(part.dtype)
        flying[0, c] = remote(
            part.at[other_half, cols], got1.at[:, cols], sum_send.at[0, c], sum_recv.at[0, c], near
        )

    def halve(c):
        cols = cols_of(c)
        flying[0, c].wait_recv()
        part[mine_half, cols] = part[mine_half, cols] + got1[:, cols]
        flying[1, c] = remote(
            part.at[other, cols], got2.at[:, cols], sum_send.at[1, c], sum_recv.at[1, c], far
        )

    def make_error(c):
        cols = cols_of(c)
        if c == 0:
            for copy in res_copies:
                copy.wait_recv()
        flying[1, c].wait_recv()
        recon = part[mine, cols] + got2[:, cols]
        shift = bias_ref[:, span(q * width + c * step, step)]
        err[mine, cols] = (recon + shift - res[:, cols].astype(jnp.float32)).astype(jnp.bfloat16)
        flying[2, c] = remote(
            err.at[mine, cols], err.at[mine, cols], sum_send.at[2, c], sum_recv.at[2, c], far
        )

    def spread(c):
        cols = cols_of(c)
        flying[2, c].wait_recv()
        flying[3, c] = remote(
            err.at[mine_half, cols],
            err.at[mine_half, cols],
            sum_send.at[3, c],
            sum_recv.at[3, c],
            near,
        )

    wg_copies = []
    wg_local = []

    def gradients(c):
        cols = cols_of(c)
        flying[3, c].wait_recv()
        wg[:, cols] = jnp.dot(
            codes_t[...], err[:, cols], preferred_element_type=jnp.float32
        ).astype(jnp.bfloat16)
        place = span(q * width + c * step, step)
        for r in range(1, QUARTERS):
            wg_copies.append(
                remote(
                    wg.at[span(mates[r] * feat, feat), cols],
                    wg_out.at[:, place],
                    wg_send.at[c, r],
                    wg_recv.at[c, r],
                    z * QUARTERS + mates[r],
                )
            )
        local = pltpu.make_async_copy(
            wg.at[span(q * feat, feat), cols], wg_out.at[:, place], wg_own.at[c]
        )
        local.start()
        wg_local.append(local)
        term = lax.dot_general(
            err[:, cols],
            dec[:, cols],
            (((1,), (1,)), ((), ())),
            preferred_element_type=jnp.float32,
        )
        back[...] = term if c == 0 else back[...] + term

    def transpose_codes():
        for f in range(QUARTERS):
            codes_t[f * feat : (f + 1) * feat, :] = (
                codes[:, f * feat : (f + 1) * feat].astype(jnp.float32).T.astype(jnp.bfloat16)
            )

    stages = (project, halve, make_error, spread, gradients)
    for tick in range(CHUNKS + LAGS[-1]):
        if tick == 1:
            transpose_codes()
        for lag, stage in zip(LAGS, stages):
            if 0 <= tick - lag < CHUNKS:
                stage(tick - lag)
    sends += list(flying.values()) + wg_copies

    @pl.loop(0, DEVICES)
    def _(i):
        rows = pl.ds(pl.multiple_of(i * rows8, rows8), rows8)
        ids8 = ids_ref[rows, :] - first
        lane = lax.broadcasted_iota(jnp.int32, (rows8, lanes), 1)
        row = row_of(i)
        value = jnp.zeros((rows8, lanes), jnp.float32)
        for f in range(plane_feat // lanes):
            at = ids8 - f * lanes
            inside = (at >= 0) & (at < lanes)
            at = jnp.clip(at, 0, lanes - 1)
            taken = []
            for batch in range(2):
                block = back[
                    pl.ds(pl.multiple_of(row + batch * rows8, rows8), rows8),
                    f * lanes : (f + 1) * lanes,
                ]
                taken.append(
                    jnp.take_along_axis(block, at, axis=1, mode="promise_in_bounds")
                )
            found = jnp.where(lane < top_k, taken[0], taken[1])
            value = jnp.where(inside, found, value)
        pick[rows, :] = value

    to_owner = []
    for r in range(1, DEVICES):
        owner = lax.rem(me + r, DEVICES)
        to_owner.append(
            remote(
                pick.at[span(owner * rows8, rows8), :],
                cg_got.at[r],
                cg_send.at[0, r],
                cg_recv.at[0, r],
                owner,
            )
        )
    for copy in to_owner:
        copy.wait_recv()
    my_rows = span(me * rows8, rows8)
    total = pick[my_rows, :]
    for r in range(1, DEVICES):
        total = total + cg_got[r]
    cg_out[my_rows, :] = total
    to_all = []
    for r in range(1, DEVICES):
        to_all.append(
            remote(
                cg_out.at[my_rows, :],
                cg_out.at[my_rows, :],
                cg_send.at[1, r],
                cg_recv.at[1, r],
                lax.rem(me + r, DEVICES),
            )
        )
    for copy in to_all + wg_copies:
        copy.wait_recv()
    for copy in wg_local:
        copy.wait()
    for copy in sends + to_owner + to_all:
        copy.wait_send()


def fused(residual, feature_ids, activations, decoder, bias):
    feat, model_width = decoder.shape
    batches, share_rows = residual.shape[0], residual.shape[1]
    tokens = feature_ids.shape[1]
    width = model_width // QUARTERS
    rows = batches * tokens
    ids = jnp.concatenate([feature_ids[0], feature_ids[1]], axis=1)
    acts = jnp.concatenate([activations[0], activations[1]], axis=1).astype(jnp.float32)
    lanes = ids.shape[1]
    vmem = pl.BlockSpec(memory_space=pltpu.VMEM)
    hbm = pl.BlockSpec(memory_space=pl.ANY)
    weight_grad, grads = pl.pallas_call(
        fused_kernel,
        out_shape=(
            jax.ShapeDtypeStruct((feat, model_width), jnp.bfloat16),
            jax.ShapeDtypeStruct((tokens, lanes), jnp.float32),
        ),
        in_specs=[vmem, vmem, hbm, hbm, vmem],
        out_specs=(hbm, vmem),
        scratch_shapes=[
            pltpu.VMEM((QUARTERS * feat, width), jnp.bfloat16),
            pltpu.VMEM((rows, width), SUM_TYPE),
            pltpu.VMEM((rows // 2, width), SUM_TYPE),
            pltpu.VMEM((rows // 4, width), SUM_TYPE),
            pltpu.VMEM((rows, width), jnp.bfloat16),
            pltpu.VMEM((QUARTERS * feat, width), jnp.bfloat16),
            pltpu.VMEM((rows // 4, width), jnp.bfloat16),
            pltpu.VMEM((rows, QUARTERS * feat), jnp.bfloat16),
            pltpu.VMEM((QUARTERS * feat, rows), jnp.bfloat16),
            pltpu.VMEM((rows, QUARTERS * feat), jnp.float32),
            pltpu.VMEM((tokens, lanes), jnp.float32),
            pltpu.VMEM((DEVICES, share_rows, lanes), jnp.float32),
            pltpu.SemaphoreType.DMA((2,)),
            pltpu.SemaphoreType.DMA((CHUNKS, QUARTERS)),
            pltpu.SemaphoreType.DMA((CHUNKS, QUARTERS)),
            pltpu.SemaphoreType.DMA((QUARTERS,)),
            pltpu.SemaphoreType.DMA((QUARTERS,)),
            pltpu.SemaphoreType.DMA((4, CHUNKS)),
            pltpu.SemaphoreType.DMA((4, CHUNKS)),
            pltpu.SemaphoreType.DMA((CHUNKS, QUARTERS)),
            pltpu.SemaphoreType.DMA((CHUNKS, QUARTERS)),
            pltpu.SemaphoreType.DMA((CHUNKS,)),
            pltpu.SemaphoreType.DMA((2, DEVICES)),
            pltpu.SemaphoreType.DMA((2, DEVICES)),
        ],
        compiler_params=pltpu.CompilerParams(
            collective_id=0, has_side_effects=True, vmem_limit_bytes=40 * 2**20
        ),
        name="fused_backward",
    )(
        ids,
        acts,
        residual.reshape(batches * share_rows, model_width),
        decoder,
        bias.astype(jnp.float32).reshape(1, model_width),
    )
    code_grad = grads.reshape(tokens, batches, lanes // batches).transpose(1, 0, 2)
    return weight_grad, code_grad


def local_codes(ids_block, acts_block, first_feature, feat_count):
    matches = (ids_block - first_feature)[:, :, None] == lax.iota(jnp.int32, feat_count)[
        None, None, :
    ]
    dense = jnp.einsum(
        "tkf,tk->tf", matches.astype(jnp.bfloat16), acts_block, preferred_element_type=jnp.float32
    )
    return dense.astype(jnp.bfloat16)


def pick_owned(backward, ids_block, first_feature, feat_count):
    local_ids = ids_block - first_feature
    owned = (local_ids >= 0) & (local_ids < feat_count)
    taken = jnp.take_along_axis(backward, jnp.clip(local_ids, 0, feat_count - 1), axis=1)
    return jnp.where(owned, taken, jnp.float32(0.0))


def error_products(codes, errors_all, decoder):
    weight_term = jnp.einsum("tf,td->fd", codes, errors_all, preferred_element_type=jnp.float32)
    backward = jnp.einsum("td,fd->tf", errors_all, decoder, preferred_element_type=jnp.float32)
    return (weight_term, backward)


def local(residual, feature_ids, activations, decoder, bias):
    feat_count, model_width = decoder.shape
    batches, share_rows = (residual.shape[0], residual.shape[1])
    first_feature = lax.axis_index("feat") * feat_count
    bias_wide = bias.astype(jnp.float32)
    accum = jnp.zeros((feat_count, model_width), jnp.float32)
    codes_list = [
        local_codes(feature_ids[batch], activations[batch], first_feature, feat_count)
        for batch in range(batches)
    ]
    picks = []
    for batch in range(batches):
        codes = codes_list[batch]

        def project(begin, number, codes=codes):
            return jnp.dot(codes, decoder, preferred_element_type=jnp.float32)

        recon = lax.psum_scatter(
            project(jnp.int32(0), share_rows * lax.axis_size("feat")),
            "feat",
            scatter_dimension=0,
            tiled=True,
        )
        error_share = (recon + bias_wide - residual[batch].astype(jnp.float32)).astype(jnp.bfloat16)
        errors_all = lax.all_gather(error_share, "feat", axis=0, tiled=True)
        weight_term, backward = error_products(codes, errors_all, decoder)
        accum = accum + weight_term
        picks.append(pick_owned(backward, feature_ids[batch], first_feature, feat_count))
    code_grad = lax.psum(jnp.stack(picks), "feat")
    return (accum.astype(jnp.bfloat16), code_grad)


def solution(mesh):
    placed = (
        P(None, ("groups", "feat"), None),
        P(None, "groups", None),
        P(None, "groups", None),
        P(("groups", "feat"), None),
        P("groups"),
    )
    return jax.shard_map(
        fused if mesh.shape["feat"] == DEVICES else local,
        mesh=mesh,
        in_specs=placed,
        out_specs=(P(("groups", "feat"), None), P(None, "groups", None)),
        check_vma=False,
    )
```

```python
import jax
import jax.numpy as jnp
from jax import lax
from jax.experimental import pallas as pl
from jax.experimental.pallas import tpu as pltpu
from jax.sharding import PartitionSpec as P

MESH = pl.DeviceIdType.MESH
PLANES = 4
QUARTERS = 4
DEVICES = PLANES * QUARTERS
CHUNKS = 8
LAGS = (0, 1, 2, 3, 4, 5, 6)
SUM_TYPE = jnp.float32


def fused_kernel(
    ids_ref,
    acts_ref,
    res_ref,
    dec_in,
    bias_ref,
    wg_out,
    cg_out,
    dec,
    part,
    got1,
    got2,
    got3,
    err,
    wg,
    res,
    codes,
    codes_t,
    back,
    pick,
    cg_got,
    own_sem,
    dec_send,
    dec_recv,
    res_send,
    res_recv,
    sum_send,
    sum_recv,
    wg_send,
    wg_recv,
    wg_own,
    cg_send,
    cg_recv,
):
    feat = dec_in.shape[0]
    width = dec_in.shape[1] // QUARTERS
    step = width // CHUNKS
    tokens = codes.shape[0]
    half, quarter = tokens // 2, tokens // 4
    share = res_ref.shape[0]
    lanes = ids_ref.shape[1]
    top_k = lanes // 2
    rows8 = share // 2

    me = lax.axis_index("feat")
    z, q = lax.div(me, QUARTERS), lax.rem(me, QUARTERS)
    side, z_lo = lax.div(z, 2), lax.rem(z, 2)
    inner = lax.rem(z_lo + side, 2)
    near = (z + 1 - 2 * z_lo) * QUARTERS + q
    across = (PLANES - 1 - z) * QUARTERS + q
    mates = [lax.rem(q + r, QUARTERS) for r in range(QUARTERS)]

    def span(start, size):
        return pl.ds(pl.multiple_of(start, size), size)

    def remote(src, dst, send, recv, device):
        copy = pltpu.make_async_remote_copy(
            src_ref=src,
            dst_ref=dst,
            send_sem=send,
            recv_sem=recv,
            device_id={"feat": device},
            device_id_type=MESH,
        )
        copy.start()
        return copy

    barrier = pltpu.get_barrier_semaphore()
    for r in range(1, DEVICES):
        pl.semaphore_signal(
            barrier, inc=1, device_id={"feat": lax.rem(me + r, DEVICES)}, device_id_type=MESH
        )
    pl.semaphore_wait(barrier, DEVICES - 1)

    sends = []
    own_dec = pltpu.make_async_copy(
        dec_in.at[:, span(q * width, width)], dec.at[span(q * feat, feat), :], own_sem.at[0]
    )
    own_dec.start()
    own_res = pltpu.make_async_copy(
        res_ref.at[:, span(q * width, width)], res.at[span(q * share, share), :], own_sem.at[1]
    )
    own_res.start()
    dec_copies = {}
    res_copies = []
    for c in range(CHUNKS):
        for r in range(1, QUARTERS):
            dec_copies[c, r] = remote(
                dec_in.at[:, span(mates[r] * width + c * step, step)],
                dec.at[span(q * feat, feat), pl.ds(c * step, step)],
                dec_send.at[c, r],
                dec_recv.at[c, r],
                z * QUARTERS + mates[r],
            )
        if c == 0:
            for r in range(1, QUARTERS):
                res_copies.append(
                    remote(
                        res_ref.at[:, span(mates[r] * width, width)],
                        res.at[span(q * share, share), :],
                        res_send.at[r],
                        res_recv.at[r],
                        z * QUARTERS + mates[r],
                    )
                )
    sends += list(dec_copies.values()) + res_copies

    plane_feat = QUARTERS * feat
    first = z * plane_feat

    def row_of(i):
        zi, qi = lax.div(i, QUARTERS), lax.rem(i, QUARTERS)
        side_i = lax.div(zi, 2)
        block = side_i * 2 + lax.rem(lax.rem(zi, 2) + side_i, 2)
        return pl.multiple_of(block * quarter + qi * share, share)

    @pl.loop(0, DEVICES)
    def _(i):
        rows = pl.ds(pl.multiple_of(i * rows8, rows8), rows8)
        ids8 = ids_ref[rows, :] - first
        acts8 = acts_ref[rows, :]
        feature = lax.broadcasted_iota(jnp.int32, (rows8, plane_feat), 1)
        blocks = []
        for batch in range(2):
            block = jnp.zeros((rows8, plane_feat), jnp.float32)
            for k in range(batch * top_k, (batch + 1) * top_k):
                block = jnp.where(ids8[:, k : k + 1] == feature, acts8[:, k : k + 1], block)
            blocks.append(block)
        both = jnp.concatenate(blocks, axis=0)
        codes[pl.ds(row_of(i), share), :] = both.astype(jnp.bfloat16)

    own_dec.wait()
    own_res.wait()

    mine_half = span(side * half, half)
    other_half = span((1 - side) * half, half)
    end_rows = span(side * half, quarter)
    inner_rows = span(side * half + quarter, quarter)
    mine = span(side * half + inner * quarter, quarter)

    def cols_of(c):
        return pl.ds(c * step, step)

    def along(kind, c):
        cols = cols_of(c)
        src, dst, device = (
            (part.at[other_half, cols], got1.at[pl.ds(0, half), cols], near),
            (part.at[inner_rows, cols], got1.at[pl.ds(half, quarter), cols], near),
            (part.at[other_half, cols], got2.at[:, cols], across),
            (part.at[end_rows, cols], got3.at[:, cols], near),
            (err.at[inner_rows, cols], err.at[inner_rows, cols], across),
            (err.at[inner_rows, cols], err.at[inner_rows, cols], near),
            (err.at[end_rows, cols], err.at[end_rows, cols], near),
            (err.at[end_rows, cols], err.at[end_rows, cols], across),
            (err.at[other_half, cols], err.at[other_half, cols], near),
        )[kind]
        return pltpu.make_async_remote_copy(
            src_ref=src,
            dst_ref=dst,
            send_sem=sum_send.at[kind, c],
            recv_sem=sum_recv.at[kind, c],
            device_id={"feat": device},
            device_id_type=MESH,
        )

    SUM_HALF, SUM_INNER, SUM_ACROSS, SUM_BACK = 0, 1, 2, 3
    ERR_ACROSS, ERR_NEAR, ERR_END, ERR_END_ACROSS, ERR_REST = 4, 5, 6, 7, 8
    FROM_END = (SUM_HALF, SUM_INNER, ERR_END)
    FROM_INNER = (SUM_ACROSS, SUM_BACK, ERR_ACROSS, ERR_NEAR, ERR_END_ACROSS, ERR_REST)

    def project(c):
        cols = cols_of(c)
        for r in range(1, QUARTERS):
            dec_copies[c, r].wait_recv()
        part[:, cols] = jnp.dot(codes[...], dec[:, cols], preferred_element_type=jnp.float32)

        @pl.when(inner == 0)
        def _():
            along(SUM_HALF, c).start()
            along(SUM_INNER, c).start()

    def pass_on(c):
        cols = cols_of(c)

        @pl.when(inner == 1)
        def _():
            along(SUM_HALF, c).wait_recv()
            part[other_half, cols] = part[other_half, cols] + got1[:half, cols]
            along(SUM_ACROSS, c).start()

    def round_error(recon, c):
        cols = cols_of(c)
        shift = bias_ref[:, span(q * width + c * step, step)]
        err[mine, cols] = (recon + shift - res[:, cols].astype(jnp.float32)).astype(jnp.bfloat16)

    def finish_inner(c):
        cols = cols_of(c)
        if c == 0:
            for copy in res_copies:
                copy.wait_recv()

        @pl.when(inner == 1)
        def _():
            along(SUM_ACROSS, c).wait_recv()
            part[end_rows, cols] = part[end_rows, cols] + got2[:quarter, cols]
            along(SUM_BACK, c).start()
            along(SUM_INNER, c).wait_recv()
            round_error(part[inner_rows, cols] + got1[half:, cols] + got2[quarter:, cols], c)
            along(ERR_ACROSS, c).start()
            along(ERR_NEAR, c).start()

    def finish_end(c):
        cols = cols_of(c)

        @pl.when(inner == 0)
        def _():
            along(SUM_BACK, c).wait_recv()
            round_error(part[end_rows, cols] + got3[:, cols], c)
            along(ERR_END, c).start()

    def send_across(c):
        @pl.when(inner == 1)
        def _():
            along(ERR_END, c).wait_recv()
            along(ERR_END_ACROSS, c).start()

    def send_back(c):
        @pl.when(inner == 1)
        def _():
            along(ERR_ACROSS, c).wait_recv()
            along(ERR_END_ACROSS, c).wait_recv()
            along(ERR_REST, c).start()

    wg_copies = []
    wg_local = []

    def gradients(c):
        cols = cols_of(c)

        @pl.when(inner == 0)
        def _():
            along(ERR_NEAR, c).wait_recv()
            along(ERR_REST, c).wait_recv()

        wg[:, cols] = jnp.dot(
            codes_t[...], err[:, cols], preferred_element_type=jnp.float32
        ).astype(jnp.bfloat16)
        place = span(q * width + c * step, step)
        for r in range(1, QUARTERS):
            wg_copies.append(
                remote(
                    wg.at[span(mates[r] * feat, feat), cols],
                    wg_out.at[:, place],
                    wg_send.at[c, r],
                    wg_recv.at[c, r],
                    z * QUARTERS + mates[r],
                )
            )
        local = pltpu.make_async_copy(
            wg.at[span(q * feat, feat), cols], wg_out.at[:, place], wg_own.at[c]
        )
        local.start()
        wg_local.append(local)
        term = lax.dot_general(
            err[:, cols],
            dec[:, cols],
            (((1,), (1,)), ((), ())),
            preferred_element_type=jnp.float32,
        )
        back[...] = term if c == 0 else back[...] + term

    def transpose_codes():
        for f in range(QUARTERS):
            codes_t[f * feat : (f + 1) * feat, :] = (
                codes[:, f * feat : (f + 1) * feat].astype(jnp.float32).T.astype(jnp.bfloat16)
            )

    stages = (project, pass_on, finish_inner, finish_end, send_across, send_back, gradients)
    for tick in range(CHUNKS + LAGS[-1]):
        if tick == 1:
            transpose_codes()
        for lag, stage in zip(LAGS, stages):
            if 0 <= tick - lag < CHUNKS:
                stage(tick - lag)
    sends += wg_copies

    @pl.loop(0, DEVICES)
    def _(i):
        rows = pl.ds(pl.multiple_of(i * rows8, rows8), rows8)
        ids8 = ids_ref[rows, :] - first
        lane = lax.broadcasted_iota(jnp.int32, (rows8, lanes), 1)
        row = row_of(i)
        value = jnp.zeros((rows8, lanes), jnp.float32)
        for f in range(plane_feat // lanes):
            at = ids8 - f * lanes
            inside = (at >= 0) & (at < lanes)
            at = jnp.clip(at, 0, lanes - 1)
            taken = []
            for batch in range(2):
                block = back[
                    pl.ds(pl.multiple_of(row + batch * rows8, rows8), rows8),
                    f * lanes : (f + 1) * lanes,
                ]
                taken.append(
                    jnp.take_along_axis(block, at, axis=1, mode="promise_in_bounds")
                )
            found = jnp.where(lane < top_k, taken[0], taken[1])
            value = jnp.where(inside, found, value)
        pick[rows, :] = value

    to_owner = []
    for r in range(1, DEVICES):
        owner = lax.rem(me + r, DEVICES)
        to_owner.append(
            remote(
                pick.at[span(owner * rows8, rows8), :],
                cg_got.at[r],
                cg_send.at[0, r],
                cg_recv.at[0, r],
                owner,
            )
        )
    for copy in to_owner:
        copy.wait_recv()
    my_rows = span(me * rows8, rows8)
    total = pick[my_rows, :]
    for r in range(1, DEVICES):
        total = total + cg_got[r]
    cg_out[my_rows, :] = total
    to_all = []
    for r in range(1, DEVICES):
        to_all.append(
            remote(
                cg_out.at[my_rows, :],
                cg_out.at[my_rows, :],
                cg_send.at[1, r],
                cg_recv.at[1, r],
                lax.rem(me + r, DEVICES),
            )
        )
    for copy in to_all + wg_copies:
        copy.wait_recv()
    for copy in wg_local:
        copy.wait()
    for copy in sends + to_owner + to_all:
        copy.wait_send()

    @pl.when(inner == 0)
    def _():
        for kind in FROM_END:
            for c in range(CHUNKS):
                along(kind, c).wait_send()

    @pl.when(inner == 1)
    def _():
        for kind in FROM_INNER:
            for c in range(CHUNKS):
                along(kind, c).wait_send()


def fused(residual, feature_ids, activations, decoder, bias):
    feat, model_width = decoder.shape
    batches, share_rows = residual.shape[0], residual.shape[1]
    tokens = feature_ids.shape[1]
    width = model_width // QUARTERS
    rows = batches * tokens
    ids = jnp.concatenate([feature_ids[0], feature_ids[1]], axis=1)
    acts = jnp.concatenate([activations[0], activations[1]], axis=1).astype(jnp.float32)
    lanes = ids.shape[1]
    vmem = pl.BlockSpec(memory_space=pltpu.VMEM)
    hbm = pl.BlockSpec(memory_space=pl.ANY)
    weight_grad, grads = pl.pallas_call(
        fused_kernel,
        out_shape=(
            jax.ShapeDtypeStruct((feat, model_width), jnp.bfloat16),
            jax.ShapeDtypeStruct((tokens, lanes), jnp.float32),
        ),
        in_specs=[vmem, vmem, hbm, hbm, vmem],
        out_specs=(hbm, vmem),
        scratch_shapes=[
            pltpu.VMEM((QUARTERS * feat, width), jnp.bfloat16),
            pltpu.VMEM((rows, width), SUM_TYPE),
            pltpu.VMEM((3 * rows // 4, width), SUM_TYPE),
            pltpu.VMEM((rows // 2, width), SUM_TYPE),
            pltpu.VMEM((rows // 4, width), SUM_TYPE),
            pltpu.VMEM((rows, width), jnp.bfloat16),
            pltpu.VMEM((QUARTERS * feat, width), jnp.bfloat16),
            pltpu.VMEM((rows // 4, width), jnp.bfloat16),
            pltpu.VMEM((rows, QUARTERS * feat), jnp.bfloat16),
            pltpu.VMEM((QUARTERS * feat, rows), jnp.bfloat16),
            pltpu.VMEM((rows, QUARTERS * feat), jnp.float32),
            pltpu.VMEM((tokens, lanes), jnp.float32),
            pltpu.VMEM((DEVICES, share_rows, lanes), jnp.float32),
            pltpu.SemaphoreType.DMA((2,)),
            pltpu.SemaphoreType.DMA((CHUNKS, QUARTERS)),
            pltpu.SemaphoreType.DMA((CHUNKS, QUARTERS)),
            pltpu.SemaphoreType.DMA((QUARTERS,)),
            pltpu.SemaphoreType.DMA((QUARTERS,)),
            pltpu.SemaphoreType.DMA((9, CHUNKS)),
            pltpu.SemaphoreType.DMA((9, CHUNKS)),
            pltpu.SemaphoreType.DMA((CHUNKS, QUARTERS)),
            pltpu.SemaphoreType.DMA((CHUNKS, QUARTERS)),
            pltpu.SemaphoreType.DMA((CHUNKS,)),
            pltpu.SemaphoreType.DMA((2, DEVICES)),
            pltpu.SemaphoreType.DMA((2, DEVICES)),
        ],
        compiler_params=pltpu.CompilerParams(
            collective_id=0, has_side_effects=True, vmem_limit_bytes=40 * 2**20
        ),
        name="fused_backward",
    )(
        ids,
        acts,
        residual.reshape(batches * share_rows, model_width),
        decoder,
        bias.astype(jnp.float32).reshape(1, model_width),
    )
    code_grad = grads.reshape(tokens, batches, lanes // batches).transpose(1, 0, 2)
    return weight_grad, code_grad


def local_codes(ids_block, acts_block, first_feature, feat_count):
    matches = (ids_block - first_feature)[:, :, None] == lax.iota(jnp.int32, feat_count)[
        None, None, :
    ]
    dense = jnp.einsum(
        "tkf,tk->tf", matches.astype(jnp.bfloat16), acts_block, preferred_element_type=jnp.float32
    )
    return dense.astype(jnp.bfloat16)


def pick_owned(backward, ids_block, first_feature, feat_count):
    local_ids = ids_block - first_feature
    owned = (local_ids >= 0) & (local_ids < feat_count)
    taken = jnp.take_along_axis(backward, jnp.clip(local_ids, 0, feat_count - 1), axis=1)
    return jnp.where(owned, taken, jnp.float32(0.0))


def error_products(codes, errors_all, decoder):
    weight_term = jnp.einsum("tf,td->fd", codes, errors_all, preferred_element_type=jnp.float32)
    backward = jnp.einsum("td,fd->tf", errors_all, decoder, preferred_element_type=jnp.float32)
    return (weight_term, backward)


def local(residual, feature_ids, activations, decoder, bias):
    feat_count, model_width = decoder.shape
    batches, share_rows = (residual.shape[0], residual.shape[1])
    first_feature = lax.axis_index("feat") * feat_count
    bias_wide = bias.astype(jnp.float32)
    accum = jnp.zeros((feat_count, model_width), jnp.float32)
    codes_list = [
        local_codes(feature_ids[batch], activations[batch], first_feature, feat_count)
        for batch in range(batches)
    ]
    picks = []
    for batch in range(batches):
        codes = codes_list[batch]

        def project(begin, number, codes=codes):
            return jnp.dot(codes, decoder, preferred_element_type=jnp.float32)

        recon = lax.psum_scatter(
            project(jnp.int32(0), share_rows * lax.axis_size("feat")),
            "feat",
            scatter_dimension=0,
            tiled=True,
        )
        error_share = (recon + bias_wide - residual[batch].astype(jnp.float32)).astype(jnp.bfloat16)
        errors_all = lax.all_gather(error_share, "feat", axis=0, tiled=True)
        weight_term, backward = error_products(codes, errors_all, decoder)
        accum = accum + weight_term
        picks.append(pick_owned(backward, feature_ids[batch], first_feature, feat_count))
    code_grad = lax.psum(jnp.stack(picks), "feat")
    return (accum.astype(jnp.bfloat16), code_grad)


def solution(mesh):
    placed = (
        P(None, ("groups", "feat"), None),
        P(None, "groups", None),
        P(None, "groups", None),
        P(("groups", "feat"), None),
        P("groups"),
    )
    return jax.shard_map(
        fused if mesh.shape["feat"] == DEVICES else local,
        mesh=mesh,
        in_specs=placed,
        out_specs=(P(("groups", "feat"), None), P(None, "groups", None)),
        check_vma=False,
    )
```
